128 devices in a mesh: integral: 8 (over x, core), pair: 16 (over y, z).
Axes of the slice: x: 4, y: 4, z: 4, core: 2. Of those that a mesh axis runs over, the one named last changes fastest.
Arguments:
- t2_tiles: bfloat16 [2048, 40, 1024], P('pair', None, 'integral'), may hold values from -6 to 6
- keep_tile: int32 [40], replicated, may hold values from 0 to 63, as said below
- integrals: bfloat16 [64, 1024, 8192], P('pair', None, 'integral'), may hold values from -0.0625 to 0.0625
Outputs:
- residual: bfloat16 [2048, 8192], P('pair', 'integral')
The draws below stay inside these ranges and needn't reach their ends.
Inputs may be any that keep to these rules, and one draw needn't show every extreme that they name: `keep_tile`: 40 distinct tile numbers in no particular order; tile k lies in the integral rows of pair index k // 4; at least one pair index has all 4 of its tiles listed.
All inputs are finite; a program needn't handle non-finite values.
Results may differ from the reference program's by a relative error of at most 0.0014.
Values may be sent and summed in bfloat16 or wider, within the bound.
No kernel may reach another device: no remote copies, remote signals or barrier semaphores. Data moves between devices by JAX's collectives and lax.ppermute only.
A program may use at most 128 MiB of HBM per device.

```python
import jax
import jax.numpy as jnp
from jax import lax

TT = 1024
KT_DEV = 4
KT = 64
NKEEP = 40
OPAIRS = 2048
QW = 8192


def draw_keep_tile(key, part):
    owner_total = KT // KT_DEV
    first_key, second_key, third_key = jax.random.split(key, 3)
    full_owner = jax.random.randint(first_key, (), 0, owner_total)
    tile_ids = jnp.arange(KT, dtype=jnp.int32)
    shuffled = jax.random.permutation(second_key, KT).astype(jnp.int32)
    scores = jnp.where(tile_ids // KT_DEV == full_owner, tile_ids - KT, shuffled)
    picked = jnp.argsort(scores, stable=True)[:NKEEP]
    return picked[jax.random.permutation(third_key, NKEEP)].astype(jnp.int32)


def level_of(stream_key, extent, pieces, low, largest):
    factor_of = 1.0
    for position, blocks in pieces:
        heights = jax.random.uniform(jax.random.fold_in(jax.random.fold_in(stream_key, 6), position), (blocks,), jnp.float32, low / len(pieces), largest / len(pieces))
        factor_of = factor_of * jnp.repeat(jnp.exp(heights), extent[position] // blocks).reshape((-1,) + (1,) * (len(extent) - 1 - position))
    return factor_of


def gaussian(own_key, shape, spread, most, cuts=(), held_as=jnp.bfloat16):
    entries = jax.random.normal(own_key, shape, jnp.float32) * spread
    if len(cuts) > 0:
        entries = level_of(own_key, shape, cuts, -0.22, 0.18) * entries
    return jnp.clip(entries, min=-most, max=most).astype(held_as)


def setup_inputs(seed: int = 0) -> dict:
    seeds = jax.random.split(jax.random.key(seed), 4)
    t2_tiles = gaussian(seeds[0], (OPAIRS, NKEEP, TT), 1.0, 6.0, ((0, 16), (2, 8)))
    keep_tile = draw_keep_tile(jax.random.fold_in(seeds[3], 71), 0)
    integrals = gaussian(seeds[2], (KT, TT, QW), (NKEEP * TT // 4) ** -0.5, 0.0625, ((0, 16), (2, 8)))
    return {"t2_tiles": t2_tiles, "keep_tile": keep_tile, "integrals": integrals}


def reference(t2_tiles, keep_tile, integrals):
    def add_tile(running, inputs):
        amp_rows, tile_number = inputs
        v_rows = lax.dynamic_index_in_dim(integrals, tile_number, 0, keepdims=False)
        return running + jnp.dot(amp_rows, v_rows, preferred_element_type=jnp.float32), None

    start_sum = jnp.zeros((t2_tiles.shape[0], integrals.shape[2]), jnp.float32)
    partial_value, _ = lax.scan(add_tile, start_sum, (jnp.swapaxes(t2_tiles, 0, 1), keep_tile.astype(jnp.int32)))
    return (0.5 * partial_value).astype(jnp.bfloat16)
```

```python
import functools

import jax
import jax.numpy as jnp
import numpy as np
from jax import lax
from jax.experimental import pallas as pl
from jax.experimental.pallas import tpu as pltpu
from jax.sharding import Mesh
from jax.sharding import PartitionSpec as P

X, C, Y, Z = 4, 2, 4, 4
CHUNKS = (32, 32, 32, 32)
VMEM_LIMIT = 56 * 1024 * 1024


def shift(a, axis, by, n=4):
    return lax.ppermute(a, axis, [(i, (i + by) % n) for i in range(n)])


def pack_kernel(slots, keep_ref, t2_ref, *refs):
    outs, wide = refs[:-1], refs[-1]
    rows, kept, _ = t2_ref.shape
    wide[...] = t2_ref[...].astype(jnp.float32).reshape(wide.shape)
    for out in outs:
        out[...] = jnp.zeros_like(out)
    for j in range(kept):
        tile = keep_ref[j]
        owner, slot = tile // slots, tile % slots
        one = wide[pl.ds(j, rows, stride=kept), :].astype(jnp.bfloat16)
        first = 0
        for out in outs:
            count = out.shape[2]
            out[owner, slot] = one[first : first + count]
            first += count


def pack(t2, keep, owners, slots, chunks):
    rows, kept, cols = t2.shape
    return pl.pallas_call(
        functools.partial(pack_kernel, slots),
        out_shape=[jax.ShapeDtypeStruct((owners, slots, c, cols), t2.dtype) for c in chunks],
        in_specs=[pl.BlockSpec(memory_space=pltpu.SMEM), pl.BlockSpec(memory_space=pltpu.VMEM)],
        out_specs=[pl.BlockSpec(memory_space=pltpu.VMEM)] * len(chunks),
        scratch_shapes=[pltpu.VMEM((rows * kept, cols), jnp.float32)],
        compiler_params=pltpu.CompilerParams(vmem_limit_bytes=VMEM_LIMIT),
        name="pack",
    )(keep, t2)


def product_kernel(order_ref, *refs):
    pieces, b_ref, out_ref, wide = refs[:-3], refs[-3], refs[-2], refs[-1]
    groups, slots, rows, cols = pieces[0].shape
    tile = b_ref.shape[1]

    @pl.when(pl.program_id(0) == 0)
    def _():
        for i, piece in enumerate(pieces):
            for s in range(slots):
                at = pl.multiple_of(s * tile + order_ref[i] * cols, cols)
                wide[:, pl.ds(at, cols)] = piece[:, s].reshape(groups * rows, cols)

    b = b_ref[...].reshape(slots * tile, b_ref.shape[2])
    out_ref[...] = jnp.dot(wide[...], b, preferred_element_type=jnp.float32)


def product(pieces, order, integrals, step=256):
    groups, slots, rows, cols = pieces[0].shape
    _, tile, width = integrals.shape
    m, k = groups * rows, slots * tile
    whole = pl.BlockSpec(pieces[0].shape, lambda n, o: (0, 0, 0, 0))
    return pl.pallas_call(
        product_kernel,
        out_shape=jax.ShapeDtypeStruct((m, width), jnp.float32),
        grid_spec=pltpu.PrefetchScalarGridSpec(
            num_scalar_prefetch=1,
            grid=(width // step,),
            in_specs=[whole] * len(pieces) + [pl.BlockSpec((slots, tile, step), lambda n, o: (0, 0, n))],
            out_specs=pl.BlockSpec((m, step), lambda n, o: (0, n)),
            scratch_shapes=[pltpu.VMEM((m, k), integrals.dtype)],
        ),
        compiler_params=pltpu.CompilerParams(vmem_limit_bytes=VMEM_LIMIT),
        cost_estimate=pl.CostEstimate(
            flops=2 * m * k * width,
            bytes_accessed=2 * (m * k + k * width) + 4 * m * width,
            transcendentals=0,
        ),
        name="product",
    )(order, *pieces, integrals)


def on_device(t2, keep, integrals):
    slots = integrals.shape[0]
    mx, mc, my, mz = (lax.axis_index(a) for a in ("x", "c", "y", "z"))
    packed = pack(t2, keep, Y * Z, slots, CHUNKS)

    most_a = jnp.max(jnp.abs(t2)).astype(jnp.float32)
    most_b = jnp.max(jnp.abs(integrals)).astype(jnp.float32)
    most = lax.pmax(jnp.stack([most_a, most_b]), ("x", "c", "y", "z"))
    terms = slots * integrals.shape[1] * Y
    up = 15 - jnp.ceil(jnp.log2(jnp.maximum(most[0], 1e-30))) - jnp.ceil(jnp.log2(jnp.maximum(most[1], 1e-30)))
    up = jnp.clip(up - int(np.ceil(np.log2(terms))), -100, 100)
    scale, back = jnp.exp2(up), jnp.exp2(-up)

    places = [((mx + d) % X) * C + c for c in (mc, 1 - mc) for d in (0, -1, 1, 2)]
    order = jnp.stack(places).astype(jnp.int32)

    results = []
    for part in packed:
        own = lax.all_to_all(part, ("y", "z"), split_axis=0, concat_axis=0, tiled=True)
        left, right = shift(own, "x", 1), shift(own, "x", -1)
        half = own.shape[0] // 2
        far = jnp.concatenate([shift(left[:half], "x", 1), shift(right[half:], "x", -1)], axis=0)
        mine = [own, left, right, far]
        theirs = [shift(a, "c", 1, 2) for a in mine]
        partial_sum = product(mine + theirs, order, integrals)
        rows = part.shape[2]
        width = integrals.shape[2]
        scaled = (partial_sum * scale).reshape(Y, Z, rows, width)
        send = scaled.astype(jnp.float16)
        total = lax.dynamic_index_in_dim(scaled, my, 0, keepdims=False)
        for d in (1, 2, 3):
            out = lax.dynamic_index_in_dim(send, (my + d) % Y, 0, keepdims=False)
            total = total + shift(out, "y", d).astype(jnp.float32)
        result = lax.dynamic_index_in_dim(total, mz, 0, keepdims=False)
        for d in (1, 2, 3):
            out = lax.dynamic_index_in_dim(total, (mz + d) % Z, 0, keepdims=False)
            result = result + shift(out, "z", d)
        results.append(result)
    rows = jnp.concatenate(results, axis=0)
    return (rows * (0.5 * back)).astype(jnp.bfloat16)


def solution(mesh):
    fine = Mesh(mesh.devices.reshape(X, C, Y, Z), ("x", "c", "y", "z"))
    pair, integral = ("y", "z"), ("x", "c")
    placed = (P(pair, None, integral), P(), P(pair, None, integral))
    return jax.shard_map(on_device, mesh=fine, in_specs=placed, out_specs=P(pair, integral), check_vma=False)
```

```python
import functools

import jax
import jax.numpy as jnp
from jax import lax
from jax.experimental import pallas as pl
from jax.experimental.pallas import tpu as pltpu
from jax.sharding import Mesh
from jax.sharding import PartitionSpec as P

X, C, Y, Z = 4, 2, 4, 4
GROUPS = ((48,), (48, 32))
COLUMN_BLOCKS = 8
COST_DIV = 1
VMEM_LIMIT = 56 * 1024 * 1024
PRODUCT_VMEM = 40 * 1024 * 1024


def shift(a, axis, by, n=4):
    return lax.ppermute(a, axis, [(i, (i + by) % n) for i in range(n)])


def pack_kernel(slots, keep_ref, t2_ref, *refs):
    outs, wide = refs[:-1], refs[-1]
    rows, kept, _ = t2_ref.shape
    wide[...] = t2_ref[...].astype(jnp.float32).reshape(wide.shape)
    for out in outs:
        out[...] = jnp.zeros_like(out)
    for j in range(kept):
        tile = keep_ref[j]
        owner, slot = tile // slots, tile % slots
        one = wide[pl.ds(j, rows, stride=kept), :].astype(jnp.bfloat16)
        first = 0
        for out in outs:
            count = out.shape[2]
            out[owner, slot] = one[first : first + count]
            first += count


def pack(t2, keep, owners, slots, chunks):
    rows, kept, cols = t2.shape
    return pl.pallas_call(
        functools.partial(pack_kernel, slots),
        out_shape=[jax.ShapeDtypeStruct((owners, slots, c, cols), t2.dtype) for c in chunks],
        in_specs=[pl.BlockSpec(memory_space=pltpu.SMEM), pl.BlockSpec(memory_space=pltpu.VMEM)],
        out_specs=[pl.BlockSpec(memory_space=pltpu.VMEM)] * len(chunks),
        scratch_shapes=[pltpu.VMEM((rows * kept, cols), jnp.float32)],
        compiler_params=pltpu.CompilerParams(vmem_limit_bytes=VMEM_LIMIT),
        name="pack",
    )(keep, t2)


def product_kernel(first, halves, order_ref, *refs):
    arrays, (b_ref, out_ref, a_in, b_in, acc, sems) = list(refs[:-6]), refs[-6:]
    count, groups, slots, rows, cols = a_in.shape
    steps, deep, width = b_in.shape
    each = count // steps
    copies = []
    for i in range(count):
        t, u = i // each, i % each
        now = []
        for s in range(slots):
            span = pl.ds((u * slots + s) * cols, cols)
            at = pl.multiple_of(order_ref[i] * cols, cols)
            now.append(pltpu.make_async_copy(b_ref.at[s, pl.ds(at, cols), :], b_in.at[t, span, :], sems.at[i, s]))
        got = [arrays.pop(0)] if i not in halves else [arrays.pop(0), arrays.pop(0)]
        some = groups // len(got)
        for h, array in enumerate(got):
            begin = first if array.shape[2] > rows else 0
            source = array.at[:, :, begin : begin + rows, :]
            now.append(pltpu.make_async_copy(source, a_in.at[i, pl.ds(h * some, some)], sems.at[i, slots + h]))
        for copy in now:
            copy.start()
        copies.append(now)
    for t in range(steps):
        for now in copies[t * each : (t + 1) * each]:
            for copy in now:
                copy.wait()

        def some_columns(n, carry):
            span = pl.ds(pl.multiple_of(n * 256, 256), 256)
            a = jnp.concatenate(
                [a_in[t * each + u, :, s].reshape(groups * rows, cols) for u in range(each) for s in range(slots)], axis=1
            )
            term = jnp.dot(a, b_in[t, :, span], preferred_element_type=jnp.float32)
            if t > 0:
                term += acc[:, span]
            acc[:, span] = term
            if t == steps - 1:
                carry = jnp.maximum(carry, jnp.max(jnp.abs(term), axis=(0, 1), keepdims=True))
            return carry

        most = lax.fori_loop(0, width // 256, some_columns, jnp.zeros((1, 1), jnp.float32))
    up = 13 - jnp.floor(jnp.log2(jnp.broadcast_to(jnp.maximum(most, 2.0**-100), (8, 128))))
    scale = jnp.exp2(up)[:1]
    for n in range(width // 128):
        part = acc[:, n * 128 : (n + 1) * 128] * scale
        out_ref[:, n * rows : (n + 1) * rows, :] = part.reshape(groups, rows, 128)
    out_ref[:, width // 128 * rows :, :] = jnp.broadcast_to(up[None], (groups, 8, 128))


def product(pieces, order, integrals, first, rows, each=2):
    slots, tile, width = integrals.shape
    count, groups, cols = len(pieces), Y * Z, tile // (X * C)
    halves = tuple(i for i, piece in enumerate(pieces) if len(piece) == 2)
    arrays = [a for piece in pieces for a in piece]
    m, k = groups * rows, slots * tile
    steps = count // each
    deep = each * slots * cols
    return pl.pallas_call(
        functools.partial(product_kernel, first, halves),
        out_shape=jax.ShapeDtypeStruct((groups, width // 128 * rows + 8, 128), jnp.float32),
        in_specs=[pl.BlockSpec(memory_space=pltpu.SMEM)] + [pl.BlockSpec(memory_space=pl.ANY)] * (len(arrays) + 1),
        out_specs=pl.BlockSpec(memory_space=pltpu.VMEM),
        scratch_shapes=[
            pltpu.VMEM((count, groups, slots, rows, cols), integrals.dtype),
            pltpu.VMEM((steps, deep, width), integrals.dtype),
            pltpu.VMEM((m, width), jnp.float32),
            pltpu.SemaphoreType.DMA((count, slots + 2)),
        ],
        compiler_params=pltpu.CompilerParams(vmem_limit_bytes=PRODUCT_VMEM),
        cost_estimate=pl.CostEstimate(
            flops=2 * m * k * width // COST_DIV,
            bytes_accessed=(2 * (m * k + k * width) + 4 * m * width) // COST_DIV,
            transcendentals=0,
        ),
        name="product",
    )(order, *arrays, integrals)


def add_over_owners(sent):
    n = COLUMN_BLOCKS
    body = sent.shape[1] - 8
    rows = body // n
    got = lax.all_to_all(sent, ("y", "z"), split_axis=0, concat_axis=0, tiled=True)
    back = jnp.exp2(-got[:, body, :].astype(jnp.float32))
    total = jnp.sum(got[:, :body].astype(jnp.float32) * back[:, None, :], axis=0)
    return got, jnp.swapaxes(total.reshape(n, rows, 128), 0, 1).reshape(rows, n * 128)


def after(a, *others):
    return lax.optimization_barrier((a, *others))[0]


def swap(a):
    return shift(a, "c", 1, 2)


def on_device(t2, keep, integrals):
    slots = integrals.shape[0]
    mx, mc = lax.axis_index("x"), lax.axis_index("c")
    packed = pack(t2, keep, Y * Z, slots, [sum(g) for g in GROUPS])
    places = [((mx + d) % X) * C + c for c in (mc, 1 - mc) for d in (0, -1, 1, 2)]
    order = jnp.stack(places).astype(jnp.int32)

    results, sides, last, before = [], [], [], []
    for part, group in zip(packed, GROUPS):
        own = lax.all_to_all(part, ("y", "z"), split_axis=0, concat_axis=0, tiled=True)
        own = after(own, *sides) if sides else own
        left, right = shift(own, "x", 1), shift(own, "x", -1)
        sides = [left, right]
        near = [own, left, right]
        across = [swap(after(a, *last)) for a in near]
        first = 0
        half = own.shape[0] // 2
        for rows in group:
            span = slice(first, first + rows)
            far = [shift(left[:half, :, span], "x", 1), shift(right[half:, :, span], "x", -1)]
            far_across = [swap(after(a, *last)) for a in far]
            pieces = [[a] for a in near] + [far] + [[a] for a in across] + [far_across]
            blocks = product(pieces, order, integrals, first, rows)
            sent = blocks.astype(jnp.float16)
            last = [sent]
            got, total = add_over_owners(after(sent, *before) if before else sent)
            before = [got]
            results.append(total)
            first += rows
    return (0.5 * jnp.concatenate(results, axis=0)).astype(jnp.bfloat16)


def solution(mesh):
    fine = Mesh(mesh.devices.reshape(X, C, Y, Z), ("x", "c", "y", "z"))
    pair, integral = ("y", "z"), ("x", "c")
    placed = (P(pair, None, integral), P(), P(pair, None, integral))
    return jax.shard_map(on_device, mesh=fine, in_specs=placed, out_specs=P(pair, integral), check_vma=False)
```

```python
import functools

import jax
import jax.numpy as jnp
from jax import lax
from jax.experimental import pallas as pl
from jax.experimental.pallas import tpu as pltpu
from jax.sharding import Mesh
from jax.sharding import PartitionSpec as P

X, C, Y, Z = 4, 2, 4, 4
GROUPS = (64, 64)
BY_FAR = True
NEAR_FREE = True
COLUMN_BLOCKS = 8
STEP = 512
VMEM_LIMIT = 56 * 1024 * 1024
PRODUCT_VMEM = 40 * 1024 * 1024


def shift(a, axis, by, n=4):
    return lax.ppermute(a, axis, [(i, (i + by) % n) for i in range(n)])


def pack_kernel(slots, keep_ref, t2_ref, *refs):
    outs, wide = refs[:-1], refs[-1]
    rows, kept, _ = t2_ref.shape
    wide[...] = t2_ref[...].astype(jnp.float32).reshape(wide.shape)
    for out in outs:
        out[...] = jnp.zeros_like(out)
    for j in range(kept):
        tile = keep_ref[j]
        owner, slot = tile // slots, tile % slots
        one = wide[pl.ds(j, rows, stride=kept), :].astype(jnp.bfloat16)
        first = 0
        for out in outs:
            count = out.shape[2]
            out[owner, slot] = one[first : first + count]
            first += count


def pack(t2, keep, owners, slots, chunks):
    rows, kept, cols = t2.shape
    return pl.pallas_call(
        functools.partial(pack_kernel, slots),
        out_shape=[jax.ShapeDtypeStruct((owners, slots, c, cols), t2.dtype) for c in chunks],
        in_specs=[pl.BlockSpec(memory_space=pltpu.SMEM), pl.BlockSpec(memory_space=pltpu.VMEM)],
        out_specs=[pl.BlockSpec(memory_space=pltpu.VMEM)] * len(chunks),
        scratch_shapes=[pltpu.VMEM((rows * kept, cols), jnp.float32)],
        compiler_params=pltpu.CompilerParams(vmem_limit_bytes=VMEM_LIMIT),
        name="pack",
    )(keep, t2)


def product_kernel(halves, order_ref, *refs):
    arrays, (b_ref, out_ref, a_in, b_in, acc, sems) = list(refs[:-6]), refs[-6:]
    count, groups, slots, rows, cols = a_in.shape
    steps, deep, width = b_in.shape
    each = count // steps
    copies = []
    for i in range(count):
        t, u = i // each, i % each
        now = []
        for s in range(slots):
            span = pl.ds((u * slots + s) * cols, cols)
            at = pl.multiple_of(order_ref[i] * cols, cols)
            now.append(pltpu.make_async_copy(b_ref.at[s, pl.ds(at, cols), :], b_in.at[t, span, :], sems.at[i, s]))
        got = [arrays.pop(0)] if i not in halves else [arrays.pop(0), arrays.pop(0)]
        some = groups // len(got)
        for h, array in enumerate(got):
            now.append(pltpu.make_async_copy(array, a_in.at[i, pl.ds(h * some, some)], sems.at[i, slots + h]))
        for copy in now:
            copy.start()
        copies.append(now)
    for t in range(steps):
        for now in copies[t * each : (t + 1) * each]:
            for copy in now:
                copy.wait()

        def some_columns(n, carry):
            span = pl.ds(pl.multiple_of(n * STEP, STEP), STEP)
            a = jnp.concatenate(
                [a_in[t * each + u, :, s].reshape(groups * rows, cols) for u in range(each) for s in range(slots)], axis=1
            )
            term = jnp.dot(a, b_in[t, :, span], preferred_element_type=jnp.float32)
            if t > 0:
                term += acc[:, span]
            acc[:, span] = term
            if t == steps - 1:
                carry = jnp.maximum(carry, jnp.max(jnp.abs(term), axis=(0, 1), keepdims=True))
            return carry

        most = lax.fori_loop(0, width // STEP, some_columns, jnp.zeros((1, 1), jnp.float32))
    up = 13 - jnp.floor(jnp.log2(jnp.broadcast_to(jnp.maximum(most, 2.0**-100), (8, 128))))
    scale = jnp.exp2(up)[:1]
    for n in range(width // 128):
        part = acc[:, n * 128 : (n + 1) * 128] * scale
        out_ref[:, n * rows : (n + 1) * rows, :] = part.reshape(groups, rows, 128)
    out_ref[:, width // 128 * rows :, :] = jnp.broadcast_to(up[None], (groups, 8, 128))


def product(pieces, order, integrals, each=4):
    slots, tile, width = integrals.shape
    count = len(pieces)
    groups, _, rows, cols = pieces[0][0].shape
    halves = tuple(i for i, piece in enumerate(pieces) if len(piece) == 2)
    arrays = [a for piece in pieces for a in piece]
    m, k = groups * rows, slots * tile
    steps = count // each
    deep = each * slots * cols
    return pl.pallas_call(
        functools.partial(product_kernel, halves),
        out_shape=jax.ShapeDtypeStruct((groups, width // 128 * rows + 8, 128), jnp.float32),
        in_specs=[pl.BlockSpec(memory_space=pltpu.SMEM)] + [pl.BlockSpec(memory_space=pl.ANY)] * (len(arrays) + 1),
        out_specs=pl.BlockSpec(memory_space=pltpu.VMEM),
        scratch_shapes=[
            pltpu.VMEM((count, groups, slots, rows, cols), integrals.dtype),
            pltpu.VMEM((steps, deep, width), integrals.dtype),
            pltpu.VMEM((m, width), jnp.float32),
            pltpu.SemaphoreType.DMA((count, slots + 2)),
        ],
        compiler_params=pltpu.CompilerParams(vmem_limit_bytes=PRODUCT_VMEM),
        cost_estimate=pl.CostEstimate(
            flops=2 * m * k * width,
            bytes_accessed=2 * (m * k + k * width) + 4 * m * width,
            transcendentals=0,
        ),
        name="product",
    )(order, *arrays, integrals)


def add_over_owners(sent):
    n = COLUMN_BLOCKS
    body = sent.shape[1] - 8
    rows = body // n
    got = lax.all_to_all(sent, ("y", "z"), split_axis=0, concat_axis=0, tiled=True)
    back = jnp.exp2(-got[:, body, :].astype(jnp.float32))
    total = jnp.sum(got[:, :body].astype(jnp.float32) * back[:, None, :], axis=0)
    return got, jnp.swapaxes(total.reshape(n, rows, 128), 0, 1).reshape(rows, n * 128)


def after(a, *others):
    return lax.optimization_barrier((a, *others))[0] if others else a


def swap(a):
    return shift(a, "c", 1, 2)


def on_device(t2, keep, integrals):
    slots = integrals.shape[0]
    mx, mc = lax.axis_index("x"), lax.axis_index("c")
    packed = pack(t2, keep, Y * Z, slots, GROUPS)
    places = [((mx + d) % X) * C + c for c in (mc, 1 - mc) for d in (0, -1, 1, 2)]
    order = jnp.stack(places).astype(jnp.int32)

    owns = []
    for part in packed:
        part = after(part, *owns[-1:])
        owns.append(lax.all_to_all(part, ("y", "z"), split_axis=0, concat_axis=0, tiled=True))
    results, earlier, last, before = [], [], [], []
    for i, own in enumerate(owns):
        own = after(own, *earlier)
        left, right = shift(own, "x", 1), shift(own, "x", -1)
        half = own.shape[0] // 2
        halves = [after(a, *owns[i + 1 : i + 2]) for a in (left[:half], right[half:])]
        far = [shift(halves[0], "x", 1), shift(halves[1], "x", -1)]
        earlier = far if BY_FAR else [left, right]
        mine = [[own], [left], [right], far]
        near_held = [] if NEAR_FREE else last
        theirs = [[swap(after(a, *near_held)) for a in piece] for piece in mine[:3]]
        theirs.append([swap(after(a, *last)) for a in far])
        blocks = product(mine + theirs, order, integrals)
        sent = blocks.astype(jnp.float16)
        last = [sent]
        got, total = add_over_owners(after(sent, *before))
        before = [got]
        results.append(total)
    return (0.5 * jnp.concatenate(results, axis=0)).astype(jnp.bfloat16)


def solution(mesh):
    fine = Mesh(mesh.devices.reshape(X, C, Y, Z), ("x", "c", "y", "z"))
    pair, integral = ("y", "z"), ("x", "c")
    placed = (P(pair, None, integral), P(), P(pair, None, integral))
    return jax.shard_map(on_device, mesh=fine, in_specs=placed, out_specs=P(pair, integral), check_vma=False)
```

```python
import functools

import jax
import jax.numpy as jnp
from jax import lax
from jax.experimental import pallas as pl
from jax.experimental.pallas import tpu as pltpu
from jax.sharding import Mesh
from jax.sharding import PartitionSpec as P

X, C, Y, Z = 4, 2, 4, 4
GROUPS = ((64,), (64,))
STEP = 512
VMEM_LIMIT = 56 * 1024 * 1024
PRODUCT_VMEM = 40 * 1024 * 1024


def shift(a, axis, by, n=4):
    return lax.ppermute(a, axis, [(i, (i + by) % n) for i in range(n)])


def pack_kernel(slots, keep_ref, t2_ref, *refs):
    outs, wide = refs[:-1], refs[-1]
    rows, kept, _ = t2_ref.shape
    wide[...] = t2_ref[...].astype(jnp.float32).reshape(wide.shape)
    for out in outs:
        out[...] = jnp.zeros_like(out)
    for j in range(kept):
        tile = keep_ref[j]
        owner, slot = tile // slots, tile % slots
        one = wide[pl.ds(j, rows, stride=kept), :].astype(jnp.bfloat16)
        first = 0
        for out in outs:
            count = out.shape[2]
            out[owner, slot] = one[first : first + count]
            first += count


def pack(t2, keep, owners, slots, chunks):
    rows, kept, cols = t2.shape
    return pl.pallas_call(
        functools.partial(pack_kernel, slots),
        out_shape=[jax.ShapeDtypeStruct((owners, slots, c, cols), t2.dtype) for c in chunks],
        in_specs=[pl.BlockSpec(memory_space=pltpu.SMEM), pl.BlockSpec(memory_space=pltpu.VMEM)],
        out_specs=[pl.BlockSpec(memory_space=pltpu.VMEM)] * len(chunks),
        scratch_shapes=[pltpu.VMEM((rows * kept, cols), jnp.float32)],
        compiler_params=pltpu.CompilerParams(vmem_limit_bytes=VMEM_LIMIT),
        name="pack",
    )(keep, t2)


def product_kernel(plan, order_ref, *refs):
    arrays, (b_ref, out_ref, a_in, b_in, acc, sems) = refs[:-6], refs[-6:]
    count, groups, slots, rows, cols = a_in.shape
    steps, deep, width = b_in.shape
    each = count // steps
    copies = []
    for i in range(count):
        t, u = i // each, i % each
        now = []
        for s in range(slots):
            span = pl.ds((u * slots + s) * cols, cols)
            at = pl.multiple_of(order_ref[i] * cols, cols)
            now.append(pltpu.make_async_copy(b_ref.at[s, pl.ds(at, cols), :], b_in.at[t, span, :], sems.at[i, s]))
        some = groups // len(plan[i])
        for h, (which, lead, first) in enumerate(plan[i]):
            source = arrays[which] if lead is None else arrays[which].at[lead]
            source = source.at[:, :, pl.ds(first, rows), :]
            now.append(pltpu.make_async_copy(source, a_in.at[i, pl.ds(h * some, some)], sems.at[i, slots + h]))
        for copy in now:
            copy.start()
        copies.append(now)
    for t in range(steps):
        for now in copies[t * each : (t + 1) * each]:
            for copy in now:
                copy.wait()

        def some_columns(n, carry):
            span = pl.ds(pl.multiple_of(n * STEP, STEP), STEP)
            a = jnp.concatenate(
                [a_in[t * each + u, :, s].reshape(groups * rows, cols) for u in range(each) for s in range(slots)], axis=1
            )
            term = jnp.dot(a, b_in[t, :, span], preferred_element_type=jnp.float32)
            if t > 0:
                term += acc[:, span]
            acc[:, span] = term
            if t == steps - 1:
                carry = jnp.maximum(carry, jnp.max(jnp.abs(term), axis=(0, 1), keepdims=True))
            return carry

        most = lax.fori_loop(0, width // STEP, some_columns, jnp.zeros((1, 1), jnp.float32))
    up = 13 - jnp.floor(jnp.log2(jnp.broadcast_to(jnp.maximum(most, 2.0**-100), (8, 128))))
    scale = jnp.exp2(up)[:1]
    per = width // 256
    for n in range(2 * per):
        part = acc[:, n * 128 : (n + 1) * 128] * scale
        out_ref[:, n // per, pl.ds(n % per * rows, rows), :] = part.reshape(groups, rows, 128)
    for h in range(2):
        out_ref[:, h, pl.ds(per * rows, 8), :] = jnp.broadcast_to(up[None], (groups, 8, 128))


def product(arrays, plan, rows, order, integrals, each=4):
    slots, tile, width = integrals.shape
    count, groups, cols = len(plan), Y * Z, arrays[0].shape[-1]
    m, k = groups * rows, slots * tile
    steps = count // each
    deep = each * slots * cols
    return pl.pallas_call(
        functools.partial(product_kernel, plan),
        out_shape=jax.ShapeDtypeStruct((groups, 2, width // 256 * rows + 8, 128), jnp.float32),
        in_specs=[pl.BlockSpec(memory_space=pltpu.SMEM)] + [pl.BlockSpec(memory_space=pl.ANY)] * (len(arrays) + 1),
        out_specs=pl.BlockSpec(memory_space=pltpu.VMEM),
        scratch_shapes=[
            pltpu.VMEM((count, groups, slots, rows, cols), integrals.dtype),
            pltpu.VMEM((steps, deep, width), integrals.dtype),
            pltpu.VMEM((m, width), jnp.float32),
            pltpu.SemaphoreType.DMA((count, slots + 2)),
        ],
        compiler_params=pltpu.CompilerParams(vmem_limit_bytes=PRODUCT_VMEM),
        cost_estimate=pl.CostEstimate(
            flops=2 * m * k * width,
            bytes_accessed=2 * (m * k + k * width) + 4 * m * width,
            transcendentals=0,
        ),
        name="product",
    )(order, *arrays, integrals)


def unscaled(blocks):
    n = blocks.shape[-2] - 8
    up = blocks[..., n : n + 1, :].astype(jnp.float32)
    return blocks[..., :n, :].astype(jnp.float32) * jnp.exp2(-up)


def at_once(blocks, *before):
    sent = after(blocks.astype(jnp.float16), *before)
    got = lax.all_to_all(sent, ("y", "z"), split_axis=0, concat_axis=0, tiled=True)
    return sent, got, jnp.sum(unscaled(got), axis=0)


def as_rows(total, rows):
    n = total.shape[0] * total.shape[1] // rows
    return jnp.swapaxes(total.reshape(n, rows, 128), 0, 1).reshape(rows, n * 128)


def after(a, *others):
    return lax.optimization_barrier((a, *others))[0] if others else a


def swap(a):
    return shift(a, "c", 1, 2)


def near_pieces(own):
    return [own, shift(own, "x", 1), shift(own, "x", -1)]


def far_pieces(near, *first):
    own, left, right = near
    half = own.shape[0] // 2
    halves = [after(a, *first) for a in (left[:half], right[half:])]
    return [shift(halves[0], "x", 1), shift(halves[1], "x", -1)]


def plan_of(far_count, row):
    plan = []
    for at in (0, 3 + far_count):
        plan += [((at + d, None, row),) for d in range(3)]
        plan.append(tuple((at + 3 + h, None, row) for h in range(far_count)))
    return tuple(plan)


def on_device(t2, keep, integrals):
    slots = integrals.shape[0]
    mx, mc = lax.axis_index("x"), lax.axis_index("c")
    packed = pack(t2, keep, Y * Z, slots, [sum(g) for g in GROUPS])
    places = [((mx + d) % X) * C + c for c in (mc, 1 - mc) for d in (0, -1, 1, 2)]
    order = jnp.stack(places).astype(jnp.int32)

    owns = []
    for part in packed:
        part = after(part, *owns[-1:])
        owns.append(lax.all_to_all(part, ("y", "z"), split_axis=0, concat_axis=0, tiled=True))
    results, before, last, near = [], [], [], []
    for i, (own, group) in enumerate(zip(owns, GROUPS)):
        near = near_pieces(after(own, *near))
        far = far_pieces(near, *owns[i + 1 : i + 2])
        near_across = [swap(a) for a in near]
        arrays = near + far + near_across + [swap(after(a, *last)) for a in far]
        row = 0
        for rows in group:
            arrays = [after(a, *last) for a in arrays]
            blocks = product(arrays, plan_of(len(far), row), rows, order, integrals)
            sent, got, total = at_once(blocks, *before)
            before, last = [got], [sent]
            results.append(as_rows(total, rows))
            row += rows
    return (0.5 * jnp.concatenate(results, axis=0)).astype(jnp.bfloat16)


def solution(mesh):
    fine = Mesh(mesh.devices.reshape(X, C, Y, Z), ("x", "c", "y", "z"))
    pair, integral = ("y", "z"), ("x", "c")
    placed = (P(pair, None, integral), P(), P(pair, None, integral))
    return jax.shard_map(on_device, mesh=fine, in_specs=placed, out_specs=P(pair, integral), check_vma=False)
```
